512 devices in a mesh: dp: 16 (over x_hi, y, core), ctx: 32 (over x_lo, z).
Axes of the slice: x: 4 (x_hi: 2, x_lo: 2; x = x_hi * 2 + x_lo), y: 4, z: 16, core: 2. Of those that a mesh axis runs over, the one named last changes fastest.
Arguments:
- query: bfloat16 [16, 4096, 512], P('dp', 'ctx'), may hold values from -6 to 6
- key: bfloat16 [16, 4096, 512], P('dp', 'ctx'), may hold values from -6 to 6
- value: bfloat16 [16, 4096, 512], P('dp', 'ctx'), may hold values from -6 to 6
- out_grad: bfloat16 [16, 4096, 1024], P('dp', 'ctx'), may hold values from -6 to 6
- w_out: bfloat16 [512, 1024], P('dp'), may hold values from -0.25 to 0.25
- band_tiles: int32 [32, 3], replicated, may hold values from 0 to 1, as said below
- global_blocks: int32 [3], replicated, may hold values from 0 to 31, as said below
Outputs:
- query_grad: bfloat16 [16, 4096, 512], P('dp', 'ctx')
- key_grad: bfloat16 [16, 4096, 512], P('dp', 'ctx')
- value_grad: bfloat16 [16, 4096, 512], P('dp', 'ctx')
- w_out_grad: float32 [512, 1024], P(('dp', 'ctx'))
The draws below stay inside these ranges and needn't reach their ends.
Inputs may be any that keep to these rules, and one draw needn't show every extreme that they name: band_tiles[a, c] = 1 lists the tile of query block a and key block a + c - 1; column 1 is 1 in every row; entries that point outside the utterance are ignored. `global_blocks`: distinct block numbers; 0 and 31 are among them.
All inputs are finite; a program needn't handle non-finite values.
Results may differ from the reference program's by a relative error of at most 0.03.
Values may be sent and summed in bfloat16 or wider, within the bound.
No kernel may reach another device: no remote copies, remote signals or barrier semaphores. Data moves between devices by JAX's collectives and lax.ppermute only.
A program may use at most 64 MiB of HBM per device.

```python
import jax
import jax.numpy as jnp
from jax import lax

DM = 1024
HEADS = 4
HDIM = 128
BLK = 128
NGLOB = 3
HD = 512
BAND = 1
LEN = 4096
NBLK = 32
BATCH = 16


def draw_query(key, part):
    shape = (BATCH, LEN, HEADS * HDIM)
    values = jnp.clip(jax.random.normal(jax.random.fold_in(key, 2), shape, jnp.float32), -6.0, 6.0)
    return values.astype(jnp.bfloat16)


def draw_key(key, part):
    shape = (BATCH, LEN, HEADS * HDIM)
    values = jnp.clip(jax.random.normal(jax.random.fold_in(key, 3), shape, jnp.float32), -6.0, 6.0)
    return values.astype(jnp.bfloat16)


def draw_band_tiles(key, part):
    bits = jax.random.randint(jax.random.fold_in(key, 7), (NBLK, 2 * BAND + 1), 0, 2, dtype=jnp.int32)
    column = jnp.arange(2 * BAND + 1, dtype=jnp.int32)[None, :]
    return jnp.where(column == BAND, 1, bits).astype(jnp.int32)


def draw_global_blocks(key, part):
    middle = jax.random.permutation(jax.random.fold_in(key, 9), NBLK - 2)[:NGLOB - 2].astype(jnp.int32) + 1
    return jnp.concatenate([jnp.zeros((1,), jnp.int32), middle, jnp.full((1,), NBLK - 1, jnp.int32)])


def level_of(rng, shape, split, low, top_value):
    gain, own = 1.0, jax.random.fold_in(rng, 6)
    for position, parts in split:
        draws = jnp.exp(jax.random.uniform(jax.random.fold_in(own, position), (parts,), jnp.float32, low / len(split), top_value / len(split)))
        gain = gain * jnp.repeat(draws, shape[position] // parts).reshape([-1 if axis == position else 1 for axis in range(len(shape))])
    return gain


def scatter_about(own_key, extent, scale, reach, shards=(), held_as=jnp.bfloat16):
    entries = jax.random.normal(own_key, extent, jnp.float32) * scale
    if len(shards) > 0:
        entries = level_of(own_key, extent, shards, -0.22, 0.18) * entries
    return jnp.clip(entries, min=-reach, max=reach).astype(held_as)


def setup_inputs(seed: int = 0) -> dict:
    seeds = jax.random.split(jax.random.key(seed), 8)
    return {
        "query": draw_query(jax.random.fold_in(seeds[7], 71), 0),
        "key": draw_key(jax.random.fold_in(seeds[7], 71), 0),
        "value": scatter_about(seeds[2], (BATCH, LEN, HD), 1.0, 6.0, ((0, 16), (1, 32))),
        "out_grad": scatter_about(seeds[3], (BATCH, LEN, DM), 1.0, 6.0, ((0, 16), (1, 32))),
        "w_out": scatter_about(seeds[4], (HD, DM), HD ** -0.5, 0.25, ((0, 16),)),
        "band_tiles": draw_band_tiles(jax.random.fold_in(seeds[7], 71), 0),
        "global_blocks": draw_global_blocks(jax.random.fold_in(seeds[7], 71), 0),
    }


def tile_mask(band_tiles, global_blocks, q_first, q_count, k_first, k_count, n_blocks, band, blk):
    q_ids = q_first + jnp.arange(q_count, dtype=jnp.int32)
    k_ids = k_first + jnp.arange(k_count, dtype=jnp.int32)
    offset = k_ids[None, :] - q_ids[:, None]
    inside = (jnp.abs(offset) <= band) & (k_ids[None, :] >= 0) & (k_ids[None, :] < n_blocks)
    inside = inside & (q_ids[:, None] >= 0) & (q_ids[:, None] < n_blocks)
    table_hit = (q_ids[:, None] == jnp.arange(n_blocks, dtype=jnp.int32)[None, :]).astype(jnp.int32)
    rows_of = jnp.dot(table_hit, band_tiles)
    column = offset + band
    slots = jnp.arange(2 * band + 1, dtype=jnp.int32)
    chosen = jnp.sum(rows_of[:, None, :] * (column[:, :, None] == slots[None, None, :]).astype(jnp.int32), axis=2)
    shared = jnp.any(k_ids[:, None] == global_blocks[None, :], axis=1)
    tile = inside & (chosen > 0) & jnp.logical_not(shared)[None, :]
    full = jnp.broadcast_to(tile[:, None, :, None], (q_count, blk, k_count, blk))
    return full.reshape(q_count * blk, k_count * blk)


def one_sequence(items, w_out, band_tiles, global_blocks):
    query, key, value, out_grad = items
    width = HEADS * HDIM
    scale = HDIM ** -0.5
    d_out = jnp.dot(out_grad, w_out.T, preferred_element_type=jnp.float32).astype(jnp.bfloat16)
    rim = BAND * BLK
    zeros = jnp.zeros((rim, width), jnp.bfloat16)
    key_pad = jnp.concatenate([zeros, key, zeros], 0)
    value_pad = jnp.concatenate([zeros, value, zeros], 0)
    glob_rows = (global_blocks[:, None] * BLK + jnp.arange(BLK, dtype=jnp.int32)[None, :]).reshape(-1)
    key_glob = key[glob_rows]
    value_glob = value[glob_rows]
    span = (2 * BAND + 1) * BLK

    def step(carry, block):
        dk_pad, dv_pad, dk_glob, dv_glob = carry
        start = (block * BLK).astype(jnp.int32)
        q_blk = lax.dynamic_slice_in_dim(query, start, BLK, 0)
        d_blk = lax.dynamic_slice_in_dim(d_out, start, BLK, 0)
        keys = jnp.concatenate([lax.dynamic_slice_in_dim(key_pad, start, span, 0), key_glob], 0)
        vals = jnp.concatenate([lax.dynamic_slice_in_dim(value_pad, start, span, 0), value_glob], 0)
        band = tile_mask(band_tiles, global_blocks, block, 1, block - BAND, 2 * BAND + 1, NBLK, BAND, BLK)
        mask = jnp.concatenate([band, jnp.ones((BLK, NGLOB * BLK), bool)], 1)
        q_heads = q_blk.astype(jnp.float32).reshape(BLK, HEADS, HDIM)
        k_heads = keys.astype(jnp.float32).reshape(-1, HEADS, HDIM)
        v_heads = vals.astype(jnp.float32).reshape(-1, HEADS, HDIM)
        d_heads = d_blk.astype(jnp.float32).reshape(BLK, HEADS, HDIM)
        scores = jnp.einsum("qhd,khd->hqk", q_heads, k_heads) * scale
        scores = jnp.where(mask[None], scores, -jnp.inf)
        peak = jnp.max(scores, axis=2, keepdims=True)
        expo = jnp.where(mask[None], jnp.exp(scores - peak), 0.0)
        prob = expo / jnp.sum(expo, axis=2, keepdims=True)
        prob_low = lax.optimization_barrier(prob.astype(jnp.bfloat16)).astype(jnp.float32)
        attended = jnp.einsum("hqk,khd->qhd", prob_low, v_heads).astype(jnp.bfloat16)
        delta = jnp.sum(d_heads * attended.astype(jnp.float32), axis=2)
        slope = jnp.einsum("qhd,khd->hqk", d_heads, v_heads)
        dscore = (prob * (slope - delta.T[:, :, None])).astype(jnp.bfloat16)
        dscore = lax.optimization_barrier(dscore).astype(jnp.float32)
        dq = (scale * jnp.einsum("hqk,khd->qhd", dscore, k_heads)).reshape(BLK, width).astype(jnp.bfloat16)
        dk_part = (scale * jnp.einsum("hqk,qhd->khd", dscore, q_heads)).reshape(-1, width)
        dv_part = jnp.einsum("hqk,qhd->khd", prob_low, d_heads).reshape(-1, width)
        dk_pad = lax.dynamic_update_slice_in_dim(dk_pad, lax.dynamic_slice_in_dim(dk_pad, start, span, 0) + dk_part[:span], start, 0)
        dv_pad = lax.dynamic_update_slice_in_dim(dv_pad, lax.dynamic_slice_in_dim(dv_pad, start, span, 0) + dv_part[:span], start, 0)
        dk_glob = dk_glob + dk_part[span:]
        dv_glob = dv_glob + dv_part[span:]
        return (dk_pad, dv_pad, dk_glob, dv_glob), (dq, attended.reshape(BLK, width))

    start_carry = (jnp.zeros((LEN + 2 * rim, width), jnp.float32), jnp.zeros((LEN + 2 * rim, width), jnp.float32),
                   jnp.zeros((NGLOB * BLK, width), jnp.float32), jnp.zeros((NGLOB * BLK, width), jnp.float32))
    carry, (dq_all, att_all) = lax.scan(step, start_carry, jnp.arange(NBLK, dtype=jnp.int32))
    dk_pad, dv_pad, dk_glob, dv_glob = carry
    dk = dk_pad[rim:rim + LEN].reshape(NBLK, BLK, width).at[global_blocks].add(dk_glob.reshape(NGLOB, BLK, width))
    dv = dv_pad[rim:rim + LEN].reshape(NBLK, BLK, width).at[global_blocks].add(dv_glob.reshape(NGLOB, BLK, width))
    attended = att_all.reshape(LEN, width)
    term = jnp.dot(attended.T, out_grad, preferred_element_type=jnp.float32)
    return (dq_all.reshape(LEN, width), dk.reshape(LEN, width).astype(jnp.bfloat16),
            dv.reshape(LEN, width).astype(jnp.bfloat16), term)


def reference(query, key, value, out_grad, w_out, band_tiles, global_blocks):
    dq, dk, dv, terms = lax.map(lambda items: one_sequence(items, w_out, band_tiles, global_blocks),
                                (query, key, value, out_grad))
    return dq, dk, dv, jnp.sum(terms, axis=0)
```

```python
import jax
import jax.numpy as jnp
from jax import lax
from jax.sharding import Mesh, PartitionSpec as P

HDIM = 128
BLK = 128
HALF = 256
NZ = 16
NCTX = 32
PIECE = 8
NGLOB = 3

UP = [(i, (i + 1) % NZ) for i in range(NZ)]
DOWN = [(i, (i - 1) % NZ) for i in range(NZ)]
SWAP = [(0, 1), (1, 0)]


def by_half(*arrays):
    low = jnp.concatenate([a[:, :HALF] for a in arrays], 1)
    high = jnp.concatenate([a[:, HALF:] for a in arrays], 1)
    return low, high


def contract_rows(left, right):
    return lax.dot_general(
        left, right, (((0,), (0,)), ((), ())), preferred_element_type=jnp.float32
    )


def contract_cols(left, right):
    return lax.dot_general(
        left, right, (((1,), (1,)), ((), ())), preferred_element_type=jnp.float32
    )


def visible_blocks(band_tiles, global_blocks, block):
    seen = []
    for column in range(3):
        other = block + column - 1
        shared = jnp.any(global_blocks == other)
        inside = (other >= 0) & (other < NCTX) & (band_tiles[block, column] > 0)
        seen.append(inside & jnp.logical_not(shared))
    return jnp.stack(seen)


def on_device(query, key, value, out_grad, w_out, band_tiles, global_blocks):
    xl = lax.axis_index("xl")
    z = lax.axis_index("z")
    core = lax.axis_index("c")
    here = xl * NZ + z
    first = xl == 0
    bf16, f32 = jnp.bfloat16, jnp.float32
    scale = HDIM ** (-0.5)
    q, k, v, grad = query[0], key[0], value[0], out_grad[0]

    w_all = lax.all_gather(w_out, ("xh", "y", "c"), axis=0, tiled=True)

    kv_low, kv_high = by_half(k, v)
    kv_mine = jnp.where(first, kv_low, kv_high)
    kv_other = lax.ppermute(jnp.where(first, kv_high, kv_low), "xl", SWAP)
    q_mine = jnp.where(first, q[:, :HALF], q[:, HALF:])
    q_send = jnp.where(first, q[:, HALF:], q[:, :HALF])
    other = lax.ppermute(jnp.concatenate([q_send, grad], 1), "xl", SWAP)
    pieces = lax.all_to_all(
        jnp.stack([kv_low, kv_high]).reshape(NCTX, PIECE, 2 * HALF), ("xl", "z"), 0, 0, tiled=True
    )
    kv = jnp.stack([kv_mine, kv_other])
    before = lax.ppermute(kv, "z", UP)
    after = lax.ppermute(kv, "z", DOWN)
    before = jnp.where(z == 0, before[::-1], before)
    after = jnp.where(z == NZ - 1, after[::-1], after)
    chosen = jnp.concatenate(
        [
            lax.dynamic_index_in_dim(pieces, global_blocks[g], 0, keepdims=False)
            for g in range(NGLOB)
        ],
        0,
    )
    shared = lax.all_to_all(
        jnp.broadcast_to(chosen[None], (NZ,) + chosen.shape), "z", 0, 0, tiled=True
    ).reshape(NGLOB * BLK, 2 * HALF)

    q2 = jnp.stack([q_mine, other[:, :HALF]])
    grad2 = jnp.stack([grad, other[:, HALF:]])
    w_mine = lax.dynamic_slice_in_dim(w_all, xl * HALF, HALF, 0)
    d_out = contract_cols(grad2.reshape(2 * BLK, -1), w_mine).astype(bf16).reshape(2, BLK, HALF)

    attended, query_parts, kv_parts = [], [], []
    for slot in range(2):
        block = here if slot == 0 else (1 - xl) * NZ + z
        seen = visible_blocks(band_tiles, global_blocks, block)
        mask = jnp.concatenate([jnp.repeat(seen, BLK), jnp.ones((NGLOB * BLK,), bool)])[None]
        keys = jnp.concatenate([before[slot], kv[slot], after[slot], shared], 0)
        outs, grads, key_grads, value_grads = [], [], [], []
        for head in range(2):
            low, high = head * HDIM, (head + 1) * HDIM
            q_head = q2[slot][:, low:high]
            d_head = d_out[slot][:, low:high]
            k_head = keys[:, low:high]
            v_head = keys[:, HALF + low : HALF + high]
            scores = jnp.where(mask, contract_cols(q_head, k_head) * scale, -jnp.inf)
            peak = jnp.max(scores, axis=1, keepdims=True)
            expo = jnp.where(mask, jnp.exp(scores - peak), 0.0)
            prob = expo / jnp.sum(expo, axis=1, keepdims=True)
            prob_low = prob.astype(bf16)
            out_head = jnp.dot(prob_low, v_head, preferred_element_type=f32).astype(bf16)
            delta = jnp.sum(d_head.astype(f32) * out_head.astype(f32), axis=1, keepdims=True)
            slope = contract_cols(d_head, v_head)
            dscore = (prob * (slope - delta)).astype(bf16)
            grads.append((scale * jnp.dot(dscore, k_head, preferred_element_type=f32)).astype(bf16))
            outs.append(out_head)
            key_grads.append(scale * contract_rows(dscore, q_head))
            value_grads.append(contract_rows(prob_low, d_head))
        attended.append(jnp.concatenate(outs, 1))
        query_parts.append(jnp.concatenate(grads, 1))
        kv_parts.append(jnp.concatenate(key_grads + value_grads, 1))

    w_part = contract_rows(jnp.concatenate(attended, 0), grad2.reshape(2 * BLK, -1))
    w_part = w_part.reshape(4, 2, 2 * NZ, w_part.shape[1])
    lower = core == 0
    w_keep = jnp.where(lower, w_part[:, 0], w_part[:, 1])
    w_send = jnp.where(lower, w_part[:, 1], w_part[:, 0]).astype(bf16)
    w_sum = w_keep + lax.ppermute(w_send, "c", SWAP).astype(f32)
    w_sum = lax.all_to_all(
        w_sum.astype(bf16).reshape(8, NZ, -1), ("y", "xh"), 0, 0, tiled=True
    )
    w_sum = jnp.sum(w_sum.astype(f32), axis=0).astype(bf16).reshape(NZ, 2, 2 * HALF)

    to_lower = jnp.stack([part[:BLK] for part in kv_parts]).astype(bf16)
    to_upper = jnp.stack([part[2 * BLK : 3 * BLK] for part in kv_parts]).astype(bf16)
    to_lower = jnp.where(z == 0, to_lower[::-1], to_lower)
    to_upper = jnp.where(z == NZ - 1, to_upper[::-1], to_upper)
    from_upper = lax.ppermute(to_lower, "z", DOWN).astype(f32)
    from_lower = lax.ppermute(to_upper, "z", UP).astype(f32)
    kv_own = [kv_parts[s][BLK : 2 * BLK] + from_upper[s] + from_lower[s] for s in range(2)]
    back = lax.ppermute(
        jnp.concatenate([query_parts[1], kv_own[1].astype(bf16)], 1), "xl", SWAP
    )

    glob_part = (kv_parts[0][3 * BLK :] + kv_parts[1][3 * BLK :]).astype(bf16)
    glob_part = glob_part.reshape(NZ, NGLOB * PIECE, 2 * HALF)
    pad = jnp.zeros((NZ, PIECE - 2, 2 * HALF), bf16)
    summed = lax.all_to_all(
        jnp.concatenate([glob_part, w_sum, pad], 1), "z", 0, 0, tiled=True
    )
    summed = jnp.sum(summed.astype(f32), axis=0)
    w_row = summed[NGLOB * PIECE : NGLOB * PIECE + 2].reshape(1, 4 * HALF)
    w_row = lax.ppermute(w_row, ("xh", "xl"), [(0, 0), (1, 2), (2, 1), (3, 3)])
    glob_sum = summed[: NGLOB * PIECE].reshape(NGLOB, PIECE, 2 * HALF)
    ids = jnp.arange(NCTX, dtype=jnp.int32)[:, None, None]
    outgoing = jnp.zeros((NCTX, PIECE, 2 * HALF), f32)
    for g in range(NGLOB):
        outgoing = jnp.where(ids == global_blocks[g], glob_sum[g][None], outgoing)
    owned = lax.all_to_all(outgoing.astype(bf16), ("xl", "z"), 0, 0, tiled=True)
    owned = owned.reshape(2, BLK, 2 * HALF).astype(f32)

    q_low = jnp.where(first, query_parts[0], back[:, :HALF])
    q_high = jnp.where(first, back[:, :HALF], query_parts[0])
    kv_back = back[:, HALF:].astype(f32)
    kv_low = (jnp.where(first, kv_own[0], kv_back) + owned[0]).astype(bf16)
    kv_high = (jnp.where(first, kv_back, kv_own[0]) + owned[1]).astype(bf16)
    query_grad = jnp.concatenate([q_low, q_high], 1)
    key_grad = jnp.concatenate([kv_low[:, :HALF], kv_high[:, :HALF]], 1)
    value_grad = jnp.concatenate([kv_low[:, HALF:], kv_high[:, HALF:]], 1)
    return query_grad[None], key_grad[None], value_grad[None], w_row


def solution(mesh):
    fine = Mesh(mesh.devices.reshape(2, 4, 2, 2, NZ), ("xh", "y", "c", "xl", "z"))
    dp, ctx = ("xh", "y", "c"), ("xl", "z")
    frames = P(dp, ctx, None)
    return jax.shard_map(
        on_device,
        mesh=fine,
        in_specs=(frames, frames, frames, frames, P(dp, None), P(), P()),
        out_specs=(frames, frames, frames, P(dp + ctx, None)),
        check_vma=False,
    )
```

```python
import jax
import jax.numpy as jnp
from jax import lax
from jax.experimental import pallas as pl
from jax.experimental.pallas import tpu as pltpu
from jax.sharding import Mesh, PartitionSpec as P

HDIM = 128
BLK = 128
HALF = 256
NZ = 16
NY = 4
NCTX = 32
PIECE = 8
NGLOB = 3
DM = 1024
SCALE = HDIM ** (-0.5)

UP = [(i, (i + 1) % NZ) for i in range(NZ)]
DOWN = [(i, (i - 1) % NZ) for i in range(NZ)]
SWAP = [(0, 1), (1, 0)]
CROSS = [(0, 0), (1, 2), (2, 1), (3, 3)]
Y_ONE = [(i, i ^ 1) for i in range(NY)]
Y_TWO = [(i, i ^ 2) for i in range(NY)]

VMEM = pl.BlockSpec(memory_space=pltpu.VMEM)
SMEM = pl.BlockSpec(memory_space=pltpu.SMEM)
ANY = pl.BlockSpec(memory_space=pl.ANY)
BF16, F32 = jnp.bfloat16, jnp.float32


def shaped(shape, dtype=BF16):
    return jax.ShapeDtypeStruct(shape, dtype)


def call(kernel, specs, operands, out_shape, scratch=(), flops=0, nbytes=2**20):
    return pl.pallas_call(
        kernel,
        out_shape=out_shape,
        in_specs=specs,
        out_specs=jax.tree.map(lambda _: VMEM, out_shape),
        scratch_shapes=scratch,
        compiler_params=pltpu.CompilerParams(vmem_limit_bytes=32 * 2**20),
        cost_estimate=pl.CostEstimate(flops=flops, bytes_accessed=nbytes, transcendentals=0),
    )(*operands)


def rows_dot(left, right):
    return lax.dot_general(left, right, (((0,), (0,)), ((), ())), preferred_element_type=F32)


def cols_dot(left, right):
    return lax.dot_general(left, right, (((1,), (1,)), ((), ())), preferred_element_type=F32)


def shard_rows(i, j):
    y = lax.axis_index("y") ^ i
    core = lax.axis_index("c") ^ j
    return pl.ds(pl.multiple_of((y * 2 + core) * NCTX, NCTX), NCTX)


def split_kernel(q_hbm, k_hbm, v_hbm, halves_ref, mine_ref, send_ref, parts, sems):
    first = lax.axis_index("xl") == 0
    copies = [
        pltpu.make_async_copy(ref, parts.at[i], sems.at[i])
        for i, ref in enumerate((k_hbm, v_hbm, q_hbm))
    ]
    for copy in copies:
        copy.start()
    for part in range(3):
        copies[part].wait()
        ref = parts.at[part]
        low, high = ref[:, :HALF], ref[:, HALF:]
        lanes = slice(part * HALF, (part + 1) * HALF)
        if part < 2:
            halves_ref[0, :, lanes] = low
            halves_ref[1, :, lanes] = high
        mine_ref[:, lanes] = jnp.where(first, low, high)
        send_ref[:, lanes] = jnp.where(first, high, low)


def stack_kernel(mine_ref, other_ref, kv_ref):
    kv_ref[0] = mine_ref[:, : 2 * HALF]
    kv_ref[1] = other_ref[:, : 2 * HALF]


def choose_kernel(globals_ref, pieces_ref, *refs):
    chosen_ref = refs[-1]
    for g in range(NGLOB):
        piece = pieces_ref[globals_ref[g]]
        for z in range(NZ):
            chosen_ref[z, :, g * 2 * HALF : (g + 1) * 2 * HALF] = piece


def project_kernel(w_ref, w_other_ref, grad_ref, grad_other_ref, d_ref, d_other_ref, w_scr):
    for j, ref in enumerate((w_ref, w_other_ref)):
        for i in range(NY):
            w_scr[shard_rows(i, j)] = ref[i * NCTX : (i + 1) * NCTX]
    d_ref[...] = cols_dot(grad_ref[...], w_scr[...]).astype(BF16)
    d_other_ref[...] = cols_dot(grad_other_ref[...], w_scr[...]).astype(BF16)


def attention_kernel(
    tiles_ref, globals_ref, mine_ref, other_ref, before_ref, after_ref, shared_ref,
    d_mine_ref, d_other_ref, grad_ref, grad_other_ref,
    dq_ref, own_ref, lower_ref, upper_ref, glob_ref, keep_ref, send_ref, attended_ref,
    projected_ref,
):
    xl = lax.axis_index("xl")
    z = lax.axis_index("z")
    for slot in range(2):
        block = (xl if slot == 0 else 1 - xl) * NZ + z
        kvq_ref = mine_ref if slot == 0 else other_ref
        d_ref = d_mine_ref if slot == 0 else d_other_ref
        below = jnp.where(z == 0, 1 - slot, slot)
        above = jnp.where(z == NZ - 1, 1 - slot, slot)
        seen = []
        for column in range(3):
            other = block + column - 1
            is_global = other == globals_ref[0]
            for g in range(1, NGLOB):
                is_global = is_global | (other == globals_ref[g])
            listed = tiles_ref[block, column] > 0
            seen.append((other >= 0) & (other < NCTX) & listed & jnp.logical_not(is_global))
        chunk = lax.broadcasted_iota(jnp.int32, (1, 6 * BLK), 1) // BLK
        mask = chunk >= 3
        for column in range(3):
            mask = mask | ((chunk == column) & seen[column])
        for head in range(2):
            lanes = slice(head * HDIM, (head + 1) * HDIM)
            v_lanes = slice(HALF + head * HDIM, HALF + (head + 1) * HDIM)
            q_lanes = slice(2 * HALF + head * HDIM, 2 * HALF + (head + 1) * HDIM)
            q_head = kvq_ref[:, q_lanes]
            d_head = d_ref[:, lanes]

            def gathered(at):
                parts = [before_ref[below, :, at], kvq_ref[:, at], after_ref[above, :, at]]
                for g in range(NGLOB):
                    start = g * 2 * HALF + at.start
                    parts.append(shared_ref[:, start : start + HDIM])
                return jnp.concatenate(parts, 0)

            keys, vals = gathered(lanes), gathered(v_lanes)
            scores = jnp.where(mask, cols_dot(q_head, keys) * SCALE, -jnp.inf)
            peak = jnp.max(scores, axis=1, keepdims=True)
            expo = jnp.exp(scores - peak)
            prob = expo / jnp.sum(expo, axis=1, keepdims=True)
            prob_low = prob.astype(BF16)
            out = jnp.dot(prob_low, vals, preferred_element_type=F32).astype(BF16)
            attended_ref[slot * BLK : (slot + 1) * BLK, lanes] = out
            delta = jnp.sum(d_head.astype(F32) * out.astype(F32), axis=1, keepdims=True)
            dscore = (prob * (cols_dot(d_head, vals) - delta)).astype(BF16)
            dq = SCALE * jnp.dot(dscore, keys, preferred_element_type=F32)
            dq_ref[slot, :, lanes] = dq.astype(BF16)
            for at, grad in (
                (lanes, SCALE * rows_dot(dscore, q_head)),
                (v_lanes, rows_dot(prob_low, d_head)),
            ):
                lower_ref[below, :, at] = grad[:BLK].astype(BF16)
                own_ref[slot, :, at] = grad[BLK : 2 * BLK]
                upper_ref[above, :, at] = grad[2 * BLK : 3 * BLK].astype(BF16)
                for g in range(NGLOB):
                    start = g * 2 * HALF + at.start
                    part = grad[(3 + g) * BLK : (4 + g) * BLK]
                    if slot == 0:
                        glob_ref[:, start : start + HDIM] = part
                    else:
                        glob_ref[:, start : start + HDIM] += part
    projected_ref[...] = rows_dot(attended_ref[:BLK], grad_ref[...])
    projected_ref[...] += rows_dot(attended_ref[BLK:], grad_other_ref[...])
    for i in range(NY):
        keep_ref[i] = projected_ref[shard_rows(i, 0)]
        send_ref[i] = projected_ref[shard_rows(i, 1)].astype(BF16)


def attention_call(*operands):
    def kernel(*refs):
        ins, outs, scratch = refs[:11], refs[11:18], refs[18:]
        glob_out, rest = outs[4], scratch
        attention_kernel(*ins, *outs[:4], rest[0], outs[5], outs[6], rest[1], rest[2])
        glob_out[...] = rest[0][...].astype(BF16)

    out_shape = (
        shaped((2, BLK, HALF)),
        shaped((2, BLK, 2 * HALF), F32),
        shaped((2, BLK, 2 * HALF)),
        shaped((2, BLK, 2 * HALF)),
        shaped((BLK, NGLOB * 2 * HALF)),
        shaped((NY, NCTX, DM), F32),
        shaped((NY, NCTX, DM)),
    )
    return pl.pallas_call(
        kernel,
        out_shape=out_shape,
        in_specs=[SMEM] * 2 + [VMEM] * 9,
        out_specs=(VMEM,) * len(out_shape),
        scratch_shapes=[
            pltpu.VMEM((BLK, NGLOB * 2 * HALF), F32),
            pltpu.VMEM((2 * BLK, HALF), BF16),
            pltpu.VMEM((HALF, DM), F32),
        ],
        compiler_params=pltpu.CompilerParams(vmem_limit_bytes=32 * 2**20),
        cost_estimate=pl.CostEstimate(
            flops=10**9, bytes_accessed=5 * 2**20, transcendentals=400000
        ),
    )(*operands)


def final_kernel(dq_ref, own_ref, upper_ref, lower_ref, back_ref, owned_ref, q_ref, k_ref, v_ref):
    first = lax.axis_index("xl") == 0
    own = own_ref[0] + upper_ref[0].astype(F32) + lower_ref[0].astype(F32)
    for half in range(2):
        mine = first if half == 0 else jnp.logical_not(first)
        back = back_ref[:, HALF:].astype(F32)
        owned = owned_ref[half * BLK : (half + 1) * BLK, : 2 * HALF].astype(F32)
        kv = (jnp.where(mine, own, back) + owned).astype(BF16)
        lanes = slice(half * HALF, (half + 1) * HALF)
        k_ref[:, lanes] = kv[:, :HALF]
        v_ref[:, lanes] = kv[:, HALF:]
        q_ref[:, lanes] = jnp.where(mine, dq_ref[0], back_ref[:, :HALF])


def on_device(query, key, value, out_grad, w_out, band_tiles, global_blocks):
    xl = lax.axis_index("xl")
    q, k, v, grad = query[0], key[0], value[0], out_grad[0]

    halves, mine, send = call(
        split_kernel,
        [ANY] * 3,
        (q, k, v),
        (shaped((2, BLK, 2 * HALF)), shaped((BLK, 3 * HALF)), shaped((BLK, 3 * HALF))),
        [pltpu.VMEM((3, BLK, 2 * HALF), BF16), pltpu.SemaphoreType.DMA((3,))],
    )
    pieces = lax.all_to_all(
        halves.reshape(NCTX, PIECE, 2 * HALF), ("xl", "z"), 0, 0, tiled=True
    )
    other = lax.ppermute(send, "xl", SWAP)
    w0 = lax.ppermute(w_out, ("xh", "xl"), CROSS)
    kv = call(stack_kernel, [VMEM] * 2, (mine, other), shaped((2, BLK, 2 * HALF)))
    before = lax.ppermute(kv, "z", UP)
    after = lax.ppermute(kv, "z", DOWN)
    w1 = lax.ppermute(w0, "y", Y_ONE)
    grad_other = lax.ppermute(grad, "xl", SWAP)
    chosen = call(
        choose_kernel,
        [SMEM, VMEM] + [ANY] * 4,
        (global_blocks, pieces, before, after, w1, grad_other),
        shaped((NZ, PIECE, NGLOB * 2 * HALF)),
    )
    shared = lax.all_to_all(chosen, "z", 0, 0, tiled=True).reshape(BLK, NGLOB * 2 * HALF)
    w01 = jnp.concatenate([w0, w1], 0)
    w_core = jnp.concatenate([w01, lax.ppermute(w01, "y", Y_TWO)], 0)
    d_mine, d_other = call(
        project_kernel,
        [VMEM] * 4,
        (w_core, lax.ppermute(w_core, "c", SWAP), grad, grad_other),
        (shaped((BLK, HALF)), shaped((BLK, HALF))),
        [pltpu.VMEM((HALF, DM), BF16)],
    )

    dq, own, to_lower, to_upper, glob, w_keep, w_send = attention_call(
        band_tiles, global_blocks, mine, other, before, after, shared,
        d_mine, d_other, grad, grad_other,
    )

    glob = lax.all_to_all(
        glob.reshape(NZ, PIECE, NGLOB * 2 * HALF), "z", 0, 0, tiled=True
    )
    w_sum = w_keep + lax.ppermute(w_send, "c", SWAP).astype(F32)
    w_sum = w_sum[:2] + lax.ppermute(w_sum[2:].astype(BF16), "y", Y_TWO).astype(F32)
    w_sum = w_sum[0] + lax.ppermute(w_sum[1].astype(BF16), "y", Y_ONE).astype(F32)
    w_sum += lax.ppermute(w_sum.astype(BF16), "xh", SWAP).astype(F32)
    w_sum = jnp.where(lax.axis_index("xh") == xl, w_sum, 0.0).astype(BF16)
    w_sum = w_sum.reshape(NCTX, PIECE, DM // PIECE)

    from_upper = lax.ppermute(to_lower, "z", DOWN)
    from_lower = lax.ppermute(to_upper, "z", UP)
    kv_other = own[1] + from_upper[1].astype(F32) + from_lower[1].astype(F32)
    back = lax.ppermute(jnp.concatenate([dq[1], kv_other.astype(BF16)], 1), "xl", SWAP)

    glob = jnp.sum(glob.astype(F32), axis=0).astype(BF16)
    ids = jnp.arange(NCTX, dtype=jnp.int32)[:, None, None]
    outgoing = jnp.zeros((NCTX, PIECE, 2 * HALF), BF16)
    for g in range(NGLOB):
        part = glob[None, :, g * 2 * HALF : (g + 1) * 2 * HALF]
        outgoing = jnp.where(ids == global_blocks[g], part, outgoing)
    owned = lax.all_to_all(
        jnp.concatenate([outgoing, w_sum], 2), ("xl", "z"), 0, 0, tiled=True
    )
    w_row = jnp.sum(owned[:, :, 2 * HALF :].astype(F32), axis=0).reshape(1, DM)
    full = shaped((BLK, 2 * HALF))
    query_grad, key_grad, value_grad = call(
        final_kernel,
        [VMEM] * 6,
        (dq, own, from_upper, from_lower, back, owned.reshape(2 * BLK, -1)),
        (full, full, full),
    )
    return query_grad[None], key_grad[None], value_grad[None], w_row


def solution(mesh):
    fine = Mesh(mesh.devices.reshape(2, NY, 2, 2, NZ), ("xh", "y", "c", "xl", "z"))
    dp, ctx = ("xh", "y", "c"), ("xl", "z")
    frames = P(dp, ctx, None)
    return jax.shard_map(
        on_device,
        mesh=fine,
        in_specs=(frames, frames, frames, frames, P(dp, None), P(), P()),
        out_specs=(frames, frames, frames, P(dp + ctx, None)),
        check_vma=False,
    )
```

```python
import jax
import jax.numpy as jnp
from jax import lax
from jax.experimental import pallas as pl
from jax.experimental.pallas import tpu as pltpu
from jax.sharding import Mesh, PartitionSpec as P

HDIM = 128
BLK = 128
HALF = 256
NZ = 16
NY = 4
NCTX = 32
PIECE = 8
NGLOB = 3
DM = 1024
SCALE = HDIM ** (-0.5)

UP = [(i, (i + 1) % NZ) for i in range(NZ)]
DOWN = [(i, (i - 1) % NZ) for i in range(NZ)]
SWAP = [(0, 1), (1, 0)]

CROSS = [(0, 0), (1, 2), (2, 1), (3, 3)]

Y_ONE = [(i, i ^ 1) for i in range(NY)]
Y_TWO = [(i, i ^ 2) for i in range(NY)]

VMEM = pl.BlockSpec(memory_space=pltpu.VMEM)
SMEM = pl.BlockSpec(memory_space=pltpu.SMEM)
ANY = pl.BlockSpec(memory_space=pl.ANY)
HBM = pl.BlockSpec(memory_space=pltpu.HBM)
BF16, F32 = jnp.bfloat16, jnp.float32


def shaped(shape, dtype=BF16):
    return jax.ShapeDtypeStruct(shape, dtype)


def call(kernel, specs, operands, out_shape, scratch=(), flops=0, nbytes=2**20, vmem=8):
    return pl.pallas_call(
        kernel,
        out_shape=out_shape,
        in_specs=specs,
        out_specs=jax.tree.map(lambda _: VMEM, out_shape),
        scratch_shapes=scratch,
        compiler_params=pltpu.CompilerParams(vmem_limit_bytes=vmem * 2**20),
        cost_estimate=pl.CostEstimate(flops=flops, bytes_accessed=nbytes, transcendentals=0),
    )(*operands)


def rows_dot(left, right):
    return lax.dot_general(left, right, (((0,), (0,)), ((), ())), preferred_element_type=F32)


def cols_dot(left, right):
    return lax.dot_general(left, right, (((1,), (1,)), ((), ())), preferred_element_type=F32)


def shard_rows(i, j):
    y = lax.axis_index("y") ^ i
    core = lax.axis_index("c") ^ j
    return pl.ds(pl.multiple_of((y * 2 + core) * NCTX, NCTX), NCTX)


def split_kernel(q_hbm, k_hbm, v_hbm, halves_ref, mine_ref, send_ref, parts, sems):
    first = lax.axis_index("xl") == 0
    copies = [
        pltpu.make_async_copy(ref, parts.at[i], sems.at[i])
        for i, ref in enumerate((k_hbm, v_hbm, q_hbm))
    ]
    for copy in copies:
        copy.start()
    for part in range(3):
        copies[part].wait()
        ref = parts.at[part]
        low, high = ref[:, :HALF], ref[:, HALF:]
        lanes = slice(part * HALF, (part + 1) * HALF)
        if part < 2:
            halves_ref[0, :, lanes] = low
            halves_ref[1, :, lanes] = high
        mine_ref[:, lanes] = jnp.where(first, low, high)
        send_ref[:, lanes] = jnp.where(first, high, low)


def is_global(globals_ref, block):
    found = block == globals_ref[0]
    for g in range(1, NGLOB):
        found = found | (block == globals_ref[g])
    return found


def place(globals_ref, g):
    block = globals_ref[g]
    second = (block >= NZ) & is_global(globals_ref, block - NZ)
    return jnp.where(block >= NZ, block - NZ, block), second


def first_slot(globals_ref):
    lower_slot = lax.axis_index("xl")
    return jnp.where(is_global(globals_ref, lax.axis_index("z")), lower_slot, 1 - lower_slot)


def stack_kernel(mine_ref, other_ref, kv_ref):
    kv_ref[0] = mine_ref[:, : 2 * HALF]
    kv_ref[1] = other_ref[:, : 2 * HALF]


def choose_kernel(globals_ref, pieces_ref, *refs):
    chosen_ref = refs[-1]
    for g in range(NGLOB):
        piece = pieces_ref[globals_ref[g]]
        for z in range(NZ):
            chosen_ref[z, :, g * 2 * HALF : (g + 1) * 2 * HALF] = piece


def project_kernel(grad_ref, grad_other_ref, w_ref, w_other_ref, d_ref, d_other_ref, w_scr):
    for j, ref in enumerate((w_ref, w_other_ref)):
        for i in range(NY):
            w_scr[shard_rows(i, j)] = ref[i * NCTX : (i + 1) * NCTX]
    d_ref[...] = cols_dot(grad_ref[...], w_scr[...]).astype(BF16)
    d_other_ref[...] = cols_dot(grad_other_ref[...], w_scr[...]).astype(BF16)


def attention_kernel(
    tiles_ref, globals_ref, mine_ref, other_ref, before_ref, after_ref, shared_ref,
    d_mine_ref, d_other_ref, grad_ref, grad_other_ref,
    dq_ref, own_ref, lower_ref, upper_ref, glob_ref, keep_ref, send_ref, attended_ref,
    projected_ref,
):
    xl = lax.axis_index("xl")
    z = lax.axis_index("z")
    for slot in range(2):
        block = (xl if slot == 0 else 1 - xl) * NZ + z
        kvq_ref = mine_ref if slot == 0 else other_ref
        d_ref = d_mine_ref if slot == 0 else d_other_ref
        below = jnp.where(z == 0, 1 - slot, slot)
        above = jnp.where(z == NZ - 1, 1 - slot, slot)
        seen = []
        for column in range(3):
            other = block + column - 1
            is_global = other == globals_ref[0]
            for g in range(1, NGLOB):
                is_global = is_global | (other == globals_ref[g])
            listed = tiles_ref[block, column] > 0
            seen.append((other >= 0) & (other < NCTX) & listed & jnp.logical_not(is_global))
        chunk = lax.broadcasted_iota(jnp.int32, (1, 6 * BLK), 1) // BLK
        mask = chunk >= 3
        for column in range(3):
            mask = mask | ((chunk == column) & seen[column])
        for head in range(2):
            lanes = slice(head * HDIM, (head + 1) * HDIM)
            v_lanes = slice(HALF + head * HDIM, HALF + (head + 1) * HDIM)
            q_lanes = slice(2 * HALF + head * HDIM, 2 * HALF + (head + 1) * HDIM)
            q_head = kvq_ref[:, q_lanes]
            d_head = d_ref[:, lanes]

            def gathered(at):
                parts = [before_ref[below, :, at], kvq_ref[:, at], after_ref[above, :, at]]
                for g in range(NGLOB):
                    start = g * 2 * HALF + at.start
                    parts.append(shared_ref[:, start : start + HDIM])
                return jnp.concatenate(parts, 0)

            keys, vals = gathered(lanes), gathered(v_lanes)
            scores = jnp.where(mask, cols_dot(q_head, keys) * SCALE, -jnp.inf)
            peak = jnp.max(scores, axis=1, keepdims=True)
            expo = jnp.exp(scores - peak)
            prob = expo / jnp.sum(expo, axis=1, keepdims=True)
            prob_low = prob.astype(BF16)
            out = jnp.dot(prob_low, vals, preferred_element_type=F32).astype(BF16)
            attended_ref[slot * BLK : (slot + 1) * BLK, lanes] = out
            delta = jnp.sum(d_head.astype(F32) * out.astype(F32), axis=1, keepdims=True)
            dscore = (prob * (cols_dot(d_head, vals) - delta)).astype(BF16)
            dq = SCALE * jnp.dot(dscore, keys, preferred_element_type=F32)
            dq_ref[slot, :, lanes] = dq.astype(BF16)
            for at, grad in (
                (lanes, SCALE * rows_dot(dscore, q_head)),
                (v_lanes, rows_dot(prob_low, d_head)),
            ):
                lower_ref[below, :, at] = grad[:BLK].astype(BF16)
                own_ref[slot, :, at] = grad[BLK : 2 * BLK]
                upper_ref[above, :, at] = grad[2 * BLK : 3 * BLK].astype(BF16)
                for g in range(NGLOB):
                    start = g * 2 * HALF + at.start
                    part = grad[(3 + g) * BLK : (4 + g) * BLK]
                    if slot == 0:
                        glob_ref[:, start : start + HDIM] = part
                    else:
                        glob_ref[:, start : start + HDIM] += part
    projected_ref[...] = rows_dot(attended_ref[:BLK], grad_ref[...])
    projected_ref[...] += rows_dot(attended_ref[BLK:], grad_other_ref[...])
    for i in range(NY):
        keep_ref[i] = projected_ref[shard_rows(i, 0)]
        send_ref[i] = projected_ref[shard_rows(i, 1)].astype(BF16)


def attention_call(*operands):
    def kernel(*refs):
        ins, outs, scratch = refs[:11], refs[11:18], refs[18:]
        glob_out, rest = outs[4], scratch
        attention_kernel(*ins, *outs[:4], rest[0], outs[5], outs[6], rest[1], rest[2])
        glob_out[...] = rest[0][...].astype(BF16)

    out_shape = (
        shaped((2, BLK, HALF)),
        shaped((2, BLK, 2 * HALF), F32),
        shaped((2, BLK, 2 * HALF)),
        shaped((2, BLK, 2 * HALF)),
        shaped((BLK, NGLOB * 2 * HALF)),
        shaped((NY, NCTX, DM), F32),
        shaped((NY, NCTX, DM)),
    )
    return pl.pallas_call(
        kernel,
        out_shape=out_shape,
        in_specs=[SMEM] * 2 + [VMEM] * 9,
        out_specs=(VMEM,) * len(out_shape),
        scratch_shapes=[
            pltpu.VMEM((BLK, NGLOB * 2 * HALF), F32),
            pltpu.VMEM((2 * BLK, HALF), BF16),
            pltpu.VMEM((HALF, DM), F32),
        ],
        compiler_params=pltpu.CompilerParams(vmem_limit_bytes=24 * 2**20),
        cost_estimate=pl.CostEstimate(
            flops=10**9, bytes_accessed=5 * 2**20, transcendentals=400000
        ),
    )(*operands)


def outgoing_kernel(globals_ref, glob_ref, w_ref, out_ref, second_ref):
    total = glob_ref[0].astype(F32)
    for z in range(1, NZ):
        total += glob_ref[z].astype(F32)
    out_ref[:, :, : 2 * HALF] = jnp.zeros((NZ, PIECE, 2 * HALF), BF16)
    out_ref[:, :, 2 * HALF :] = w_ref[...]
    second_ref[...] = jnp.zeros((NZ, PIECE, 2 * HALF), BF16)
    for g in range(NGLOB):
        part = total[:, g * 2 * HALF : (g + 1) * 2 * HALF].astype(BF16)
        column, second = place(globals_ref, g)

        @pl.when(second)
        def _():
            second_ref[column] = part

        @pl.when(jnp.logical_not(second))
        def _():
            out_ref[column, :, : 2 * HALF] = part


def combine_kernel(
    globals_ref, dq_ref, own_ref, upper_ref, lower_ref, owned_ref, second_ref, kv_ref, back_ref
):
    first = first_slot(globals_ref)
    upper_slot = 1 - lax.axis_index("xl")
    owned = owned_ref[:, : 2 * HALF].astype(F32)
    second = second_ref[...].astype(F32)
    for slot in range(2):
        total = own_ref[slot] + upper_ref[slot].astype(F32) + lower_ref[slot].astype(F32)
        total += jnp.where(first == slot, owned, 0.0)
        total += jnp.where(upper_slot == slot, second, 0.0)
        if slot == 0:
            kv_ref[...] = total.astype(BF16)
        else:
            back_ref[:, HALF:] = total.astype(BF16)
            back_ref[:, :HALF] = dq_ref[1]


def final_kernel(dq_ref, kv_ref, back_ref, q_ref, k_ref, v_ref):
    first = lax.axis_index("xl") == 0
    for half in range(2):
        mine = first if half == 0 else jnp.logical_not(first)
        lanes = slice(half * HALF, (half + 1) * HALF)
        q_ref[:, lanes] = jnp.where(mine, dq_ref[0], back_ref[:, :HALF])
        k_ref[:, lanes] = jnp.where(mine, kv_ref[:, :HALF], back_ref[:, HALF : 2 * HALF])
        v_ref[:, lanes] = jnp.where(mine, kv_ref[:, HALF:], back_ref[:, 2 * HALF :])


def over_columns(array):
    return lax.all_to_all(array.reshape(NZ, PIECE, -1), "z", 0, 0, tiled=True)


def on_device(query, key, value, out_grad, w_out, band_tiles, global_blocks):
    xl = lax.axis_index("xl")
    q, k, v, grad = query[0], key[0], value[0], out_grad[0]

    folded = global_blocks % NZ
    clash = (
        (folded[0] == folded[1]) | (folded[0] == folded[2]) | (folded[1] == folded[2])
    )
    nothing = jnp.zeros((NZ, PIECE, 2 * HALF), BF16)

    halves, mine, send = call(
        split_kernel,
        [HBM] * 3,
        (q, k, v),
        (shaped((2, BLK, 2 * HALF)), shaped((BLK, 3 * HALF)), shaped((BLK, 3 * HALF))),
        [pltpu.VMEM((3, BLK, 2 * HALF), BF16), pltpu.SemaphoreType.DMA((3,))],
        vmem=56,
    )
    pieces = lax.all_to_all(
        halves.reshape(NCTX, PIECE, 2 * HALF), ("xl", "z"), 0, 0, tiled=True
    )
    other = lax.ppermute(send, "xl", SWAP)
    grad_other = lax.ppermute(grad, "xl", SWAP)
    w0 = lax.ppermute(w_out, ("xh", "xl"), CROSS)
    w1 = lax.ppermute(w0, "y", Y_ONE)
    kv = call(stack_kernel, [VMEM] * 2, (mine, other), shaped((2, BLK, 2 * HALF)))
    before = lax.ppermute(kv, "z", UP)
    after = lax.ppermute(kv, "z", DOWN)
    chosen = call(
        choose_kernel,
        [SMEM, VMEM] + [ANY] * 4,
        (global_blocks, pieces, before, after, w1, grad_other),
        shaped((NZ, PIECE, NGLOB * 2 * HALF)),
    )
    shared = over_columns(chosen).reshape(BLK, NGLOB * 2 * HALF)
    w01 = jnp.concatenate([w0, w1], 0)
    w_core = jnp.concatenate([w01, lax.ppermute(w01, "y", Y_TWO)], 0)
    d_mine, d_other = call(
        project_kernel,
        [VMEM] * 4,
        (grad, grad_other, w_core, lax.ppermute(w_core, "c", SWAP)),
        (shaped((BLK, HALF)), shaped((BLK, HALF))),
        [pltpu.VMEM((HALF, DM), BF16)],
    )

    dq, own, to_lower, to_upper, glob, w_keep, w_send = attention_call(
        band_tiles, global_blocks, mine, other, before, after, shared,
        d_mine, d_other, grad, grad_other,
    )

    glob = over_columns(glob)
    w_sum = w_keep + lax.ppermute(w_send, "c", SWAP).astype(F32)
    w_sum = w_sum[:2] + lax.ppermute(w_sum[2:].astype(BF16), "y", Y_TWO).astype(F32)
    w_sum = w_sum[0] + lax.ppermute(w_sum[1].astype(BF16), "y", Y_ONE).astype(F32)
    lower = lax.axis_index("xh") == 0
    w_send = jnp.where(lower, w_sum[NZ:], w_sum[:NZ]).astype(BF16)
    w_sum = jnp.where(lower, w_sum[:NZ], w_sum[NZ:])
    w_sum = (w_sum + lax.ppermute(w_send, "xh", SWAP).astype(F32)).astype(BF16)
    outgoing, second = call(
        outgoing_kernel,
        [SMEM, VMEM, VMEM],
        (global_blocks, glob, w_sum.reshape(NZ, PIECE, DM // PIECE)),
        (shaped((NZ, PIECE, 2 * HALF + DM // PIECE)), shaped((NZ, PIECE, 2 * HALF))),
    )
    owned = over_columns(outgoing)
    second = lax.cond(clash, over_columns, lambda _: nothing, second)
    from_upper = lax.ppermute(to_lower, "z", DOWN)
    from_lower = lax.ppermute(to_upper, "z", UP)
    kv_mine, back = call(
        combine_kernel,
        [SMEM] + [VMEM] * 6,
        (
            global_blocks, dq, own, from_upper, from_lower,
            owned.reshape(BLK, -1), second.reshape(BLK, -1),
        ),
        (shaped((BLK, 2 * HALF)), shaped((BLK, 3 * HALF))),
    )
    w_row = jnp.sum(owned[:, :, 2 * HALF :].astype(F32), axis=0).reshape(1, DM)
    w_row = lax.ppermute(w_row, ("xh", "xl"), CROSS)
    full = shaped((BLK, 2 * HALF))
    query_grad, key_grad, value_grad = call(
        final_kernel,
        [VMEM] * 3,
        (dq, kv_mine, lax.ppermute(back, "xl", SWAP)),
        (full, full, full),
    )
    return query_grad[None], key_grad[None], value_grad[None], w_row


def solution(mesh):
    fine = Mesh(mesh.devices.reshape(2, NY, 2, 2, NZ), ("xh", "y", "c", "xl", "z"))
    dp, ctx = ("xh", "y", "c"), ("xl", "z")
    frames = P(dp, ctx, None)
    return jax.shard_map(
        on_device,
        mesh=fine,
        in_specs=(frames, frames, frames, frames, P(dp, None), P(), P()),
        out_specs=(frames, frames, frames, P(dp + ctx, None)),
        check_vma=False,
    )
```

```python
import jax
import jax.numpy as jnp
from jax import lax
from jax.experimental import pallas as pl
from jax.experimental.pallas import tpu as pltpu
from jax.sharding import Mesh, PartitionSpec as P

HDIM = 128
BLK = 128
HALF = 256
NZ = 16
NY = 4
NCTX = 32
PIECE = 8
NGLOB = 3
DM = 1024
SCALE = HDIM ** (-0.5)

UP = [(i, (i + 1) % NZ) for i in range(NZ)]
DOWN = [(i, (i - 1) % NZ) for i in range(NZ)]
SWAP = [(0, 1), (1, 0)]

CROSS = [(0, 0), (1, 2), (2, 1), (3, 3)]

Y_ONE = [(i, i ^ 1) for i in range(NY)]
Y_TWO = [(i, i ^ 2) for i in range(NY)]

VMEM = pl.BlockSpec(memory_space=pltpu.VMEM)
SMEM = pl.BlockSpec(memory_space=pltpu.SMEM)
ANY = pl.BlockSpec(memory_space=pl.ANY)
HBM = pl.BlockSpec(memory_space=pltpu.HBM)
BF16, F32 = jnp.bfloat16, jnp.float32


def shaped(shape, dtype=BF16):
    return jax.ShapeDtypeStruct(shape, dtype)


def call(kernel, specs, operands, out_shape, scratch=(), flops=0, nbytes=2**20, vmem=8):
    return pl.pallas_call(
        kernel,
        out_shape=out_shape,
        in_specs=specs,
        out_specs=jax.tree.map(lambda _: VMEM, out_shape),
        scratch_shapes=scratch,
        compiler_params=pltpu.CompilerParams(vmem_limit_bytes=vmem * 2**20),
        cost_estimate=pl.CostEstimate(flops=flops, bytes_accessed=nbytes, transcendentals=0),
    )(*operands)


def rows_dot(left, right):
    return lax.dot_general(left, right, (((0,), (0,)), ((), ())), preferred_element_type=F32)


def cols_dot(left, right):
    return lax.dot_general(left, right, (((1,), (1,)), ((), ())), preferred_element_type=F32)


def shard_rows(i, j):
    y = lax.axis_index("y") ^ i
    core = lax.axis_index("c") ^ j
    return pl.ds(pl.multiple_of((y * 2 + core) * NCTX, NCTX), NCTX)


def split_kernel(q_hbm, k_hbm, v_hbm, halves_ref, mine_ref, send_ref, parts, sems):
    first = lax.axis_index("xl") == 0
    copies = [
        pltpu.make_async_copy(ref, parts.at[i], sems.at[i])
        for i, ref in enumerate((k_hbm, v_hbm, q_hbm))
    ]
    for copy in copies:
        copy.start()
    for part in range(3):
        copies[part].wait()
        ref = parts.at[part]
        low, high = ref[:, :HALF], ref[:, HALF:]
        lanes = slice(part * HALF, (part + 1) * HALF)
        if part < 2:
            halves_ref[0, :, lanes] = low
            halves_ref[1, :, lanes] = high
        mine_ref[:, lanes] = jnp.where(first, low, high)
        send_ref[:, lanes] = jnp.where(first, high, low)


def is_global(globals_ref, block):
    found = block == globals_ref[0]
    for g in range(1, NGLOB):
        found = found | (block == globals_ref[g])
    return found


def place(globals_ref, g):
    block = globals_ref[g]
    second = (block >= NZ) & is_global(globals_ref, block - NZ)
    return jnp.where(block >= NZ, block - NZ, block), second


def first_slot(globals_ref):
    lower_slot = lax.axis_index("xl")
    return jnp.where(is_global(globals_ref, lax.axis_index("z")), lower_slot, 1 - lower_slot)


def stack_kernel(mine_ref, other_ref, kv_ref):
    kv_ref[0] = mine_ref[:, : 2 * HALF]
    kv_ref[1] = other_ref[:, : 2 * HALF]


def choose_kernel(globals_ref, pieces_ref, *refs):
    chosen_ref = refs[-1]
    for g in range(NGLOB):
        piece = pieces_ref[globals_ref[g]]
        for z in range(NZ):
            chosen_ref[z, :, g * 2 * HALF : (g + 1) * 2 * HALF] = piece


def project_kernel(grad_ref, grad_other_ref, w_ref, w_other_ref, d_ref, d_other_ref, w_scr):
    for j, ref in enumerate((w_ref, w_other_ref)):
        for i in range(NY):
            w_scr[shard_rows(i, j)] = ref[i * NCTX : (i + 1) * NCTX]
    d_ref[...] = cols_dot(grad_ref[...], w_scr[...]).astype(BF16)
    d_other_ref[...] = cols_dot(grad_other_ref[...], w_scr[...]).astype(BF16)


def attention_kernel(
    tiles_ref, globals_ref, mine_ref, other_ref, before_ref, after_ref, shared_ref,
    d_mine_ref, d_other_ref, grad_ref, grad_other_ref,
    dq_ref, own_ref, lower_ref, upper_ref, glob_ref, keep_ref, send_ref, attended_ref,
    projected_ref,
):
    xl = lax.axis_index("xl")
    z = lax.axis_index("z")
    for slot in range(2):
        block = (xl if slot == 0 else 1 - xl) * NZ + z
        kvq_ref = mine_ref if slot == 0 else other_ref
        d_ref = d_mine_ref if slot == 0 else d_other_ref
        below = jnp.where(z == 0, 1 - slot, slot)
        above = jnp.where(z == NZ - 1, 1 - slot, slot)
        seen = []
        for column in range(3):
            other = block + column - 1
            is_global = other == globals_ref[0]
            for g in range(1, NGLOB):
                is_global = is_global | (other == globals_ref[g])
            listed = tiles_ref[block, column] > 0
            seen.append((other >= 0) & (other < NCTX) & listed & jnp.logical_not(is_global))
        chunk = lax.broadcasted_iota(jnp.int32, (1, 6 * BLK), 1) // BLK
        mask = chunk >= 3
        for column in range(3):
            mask = mask | ((chunk == column) & seen[column])
        for head in range(2):
            lanes = slice(head * HDIM, (head + 1) * HDIM)
            v_lanes = slice(HALF + head * HDIM, HALF + (head + 1) * HDIM)
            q_lanes = slice(2 * HALF + head * HDIM, 2 * HALF + (head + 1) * HDIM)
            q_head = kvq_ref[:, q_lanes]
            d_head = d_ref[:, lanes]

            def gathered(at):
                parts = [before_ref[below, :, at], kvq_ref[:, at], after_ref[above, :, at]]
                for g in range(NGLOB):
                    start = g * 2 * HALF + at.start
                    parts.append(shared_ref[:, start : start + HDIM])
                return jnp.concatenate(parts, 0)

            keys, vals = gathered(lanes), gathered(v_lanes)
            scores = jnp.where(mask, cols_dot(q_head, keys) * SCALE, -jnp.inf)
            peak = jnp.max(scores, axis=1, keepdims=True)
            expo = jnp.exp(scores - peak)
            prob = expo / jnp.sum(expo, axis=1, keepdims=True)
            prob_low = prob.astype(BF16)
            out = jnp.dot(prob_low, vals, preferred_element_type=F32).astype(BF16)
            attended_ref[slot * BLK : (slot + 1) * BLK, lanes] = out
            delta = jnp.sum(d_head.astype(F32) * out.astype(F32), axis=1, keepdims=True)
            dscore = (prob * (cols_dot(d_head, vals) - delta)).astype(BF16)
            dq = SCALE * jnp.dot(dscore, keys, preferred_element_type=F32)
            dq_ref[slot, :, lanes] = dq.astype(BF16)
            for at, grad in (
                (lanes, SCALE * rows_dot(dscore, q_head)),
                (v_lanes, rows_dot(prob_low, d_head)),
            ):
                lower_ref[below, :, at] = grad[:BLK].astype(BF16)
                own_ref[slot, :, at] = grad[BLK : 2 * BLK]
                upper_ref[above, :, at] = grad[2 * BLK : 3 * BLK].astype(BF16)
                for g in range(NGLOB):
                    start = g * 2 * HALF + at.start
                    part = grad[(3 + g) * BLK : (4 + g) * BLK]
                    if slot == 0:
                        glob_ref[:, start : start + HDIM] = part
                    else:
                        glob_ref[:, start : start + HDIM] += part
    projected_ref[...] = rows_dot(attended_ref[:BLK], grad_ref[...])
    projected_ref[...] += rows_dot(attended_ref[BLK:], grad_other_ref[...])
    for i in range(NY):
        keep_ref[i] = projected_ref[shard_rows(i, 0)]
        send_ref[i] = projected_ref[shard_rows(i, 1)].astype(BF16)


def attention_call(*operands):
    def kernel(*refs):
        ins, outs, scratch = refs[:11], refs[11:18], refs[18:]
        glob_out, rest = outs[4], scratch
        attention_kernel(*ins, *outs[:4], rest[0], outs[5], outs[6], rest[1], rest[2])
        glob_out[...] = rest[0][...].astype(BF16)

    out_shape = (
        shaped((2, BLK, HALF)),
        shaped((2, BLK, 2 * HALF), F32),
        shaped((2, BLK, 2 * HALF)),
        shaped((2, BLK, 2 * HALF)),
        shaped((BLK, NGLOB * 2 * HALF)),
        shaped((NY, NCTX, DM), F32),
        shaped((NY, NCTX, DM)),
    )
    return pl.pallas_call(
        kernel,
        out_shape=out_shape,
        in_specs=[SMEM] * 2 + [VMEM] * 9,
        out_specs=(VMEM,) * len(out_shape),
        scratch_shapes=[
            pltpu.VMEM((BLK, NGLOB * 2 * HALF), F32),
            pltpu.VMEM((2 * BLK, HALF), BF16),
            pltpu.VMEM((HALF, DM), F32),
        ],
        compiler_params=pltpu.CompilerParams(vmem_limit_bytes=24 * 2**20),
        cost_estimate=pl.CostEstimate(
            flops=10**9, bytes_accessed=5 * 2**20, transcendentals=400000
        ),
    )(*operands)


def outgoing_kernel(globals_ref, glob_ref, w_ref, out_ref, second_ref):
    total = glob_ref[0].astype(F32)
    for z in range(1, NZ):
        total += glob_ref[z].astype(F32)
    out_ref[:, :, : 2 * HALF] = jnp.zeros((NZ, PIECE, 2 * HALF), BF16)
    out_ref[:, :, 2 * HALF :] = w_ref[...]
    second_ref[...] = jnp.zeros((NZ, PIECE, 2 * HALF), BF16)
    for g in range(NGLOB):
        part = total[:, g * 2 * HALF : (g + 1) * 2 * HALF].astype(BF16)
        column, second = place(globals_ref, g)

        @pl.when(second)
        def _():
            second_ref[column] = part

        @pl.when(jnp.logical_not(second))
        def _():
            out_ref[column, :, : 2 * HALF] = part


def combine_kernel(
    globals_ref, dq_ref, own_ref, upper_ref, lower_ref, owned_ref, second_ref, kv_ref, back_ref
):
    first = first_slot(globals_ref)
    upper_slot = 1 - lax.axis_index("xl")
    owned = owned_ref[:, : 2 * HALF].astype(F32)
    second = second_ref[...].astype(F32)
    for slot in range(2):
        total = own_ref[slot] + upper_ref[slot].astype(F32) + lower_ref[slot].astype(F32)
        total += jnp.where(first == slot, owned, 0.0)
        total += jnp.where(upper_slot == slot, second, 0.0)
        if slot == 0:
            kv_ref[...] = total.astype(BF16)
        else:
            back_ref[:, HALF:] = total.astype(BF16)
            back_ref[:, :HALF] = dq_ref[1]


def final_kernel(dq_ref, kv_ref, back_ref, w_ref, q_ref, k_ref, v_ref, w_out_ref):
    w_out_ref[...] = w_ref[...]
    first = lax.axis_index("xl") == 0
    for half in range(2):
        mine = first if half == 0 else jnp.logical_not(first)
        lanes = slice(half * HALF, (half + 1) * HALF)
        q_ref[:, lanes] = jnp.where(mine, dq_ref[0], back_ref[:, :HALF])
        k_ref[:, lanes] = jnp.where(mine, kv_ref[:, :HALF], back_ref[:, HALF : 2 * HALF])
        v_ref[:, lanes] = jnp.where(mine, kv_ref[:, HALF:], back_ref[:, 2 * HALF :])


def over_columns(array):
    return lax.all_to_all(array.reshape(NZ, PIECE, -1), "z", 0, 0, tiled=True)


def on_device(query, key, value, out_grad, w_out, band_tiles, global_blocks):
    xl = lax.axis_index("xl")
    q, k, v, grad = query[0], key[0], value[0], out_grad[0]

    folded = global_blocks % NZ
    clash = (
        (folded[0] == folded[1]) | (folded[0] == folded[2]) | (folded[1] == folded[2])
    )
    nothing = jnp.zeros((NZ, PIECE, 2 * HALF), BF16)

    halves, mine, send = call(
        split_kernel,
        [HBM] * 3,
        (q, k, v),
        (shaped((2, BLK, 2 * HALF)), shaped((BLK, 3 * HALF)), shaped((BLK, 3 * HALF))),
        [pltpu.VMEM((3, BLK, 2 * HALF), BF16), pltpu.SemaphoreType.DMA((3,))],
        vmem=56,
    )
    pieces = lax.all_to_all(
        halves.reshape(NCTX, PIECE, 2 * HALF), ("xl", "z"), 0, 0, tiled=True
    )
    other = lax.ppermute(send, "xl", SWAP)
    grad_other = lax.ppermute(grad, "xl", SWAP)
    w0 = lax.ppermute(w_out, ("xh", "xl"), CROSS)
    w1 = lax.ppermute(w0, "y", Y_ONE)
    kv = call(stack_kernel, [VMEM] * 2, (mine, other), shaped((2, BLK, 2 * HALF)))
    before = lax.ppermute(kv, "z", UP)
    after = lax.ppermute(kv, "z", DOWN)
    chosen = call(
        choose_kernel,
        [SMEM, VMEM] + [ANY] * 4,
        (global_blocks, pieces, before, after, w1, grad_other),
        shaped((NZ, PIECE, NGLOB * 2 * HALF)),
    )
    shared = over_columns(chosen).reshape(BLK, NGLOB * 2 * HALF)
    w01 = jnp.concatenate([w0, w1], 0)
    w_core = jnp.concatenate([w01, lax.ppermute(w01, "y", Y_TWO)], 0)
    d_mine, d_other = call(
        project_kernel,
        [VMEM] * 4,
        (grad, grad_other, w_core, lax.ppermute(w_core, "c", SWAP)),
        (shaped((BLK, HALF)), shaped((BLK, HALF))),
        [pltpu.VMEM((HALF, DM), BF16)],
    )

    dq, own, to_lower, to_upper, glob, w_keep, w_send = attention_call(
        band_tiles, global_blocks, mine, other, before, after, shared,
        d_mine, d_other, grad, grad_other,
    )

    glob = over_columns(glob)
    w_sum = w_keep + lax.ppermute(w_send, "c", SWAP).astype(F32)
    w_sum = w_sum[:2] + lax.ppermute(w_sum[2:].astype(BF16), "y", Y_TWO).astype(F32)
    w_sum = w_sum[0] + lax.ppermute(w_sum[1].astype(BF16), "y", Y_ONE).astype(F32)
    lower = lax.axis_index("xh") == 0
    w_send = jnp.where(lower, w_sum[NZ:], w_sum[:NZ]).astype(BF16)
    w_sum = jnp.where(lower, w_sum[:NZ], w_sum[NZ:])
    w_sum = (w_sum + lax.ppermute(w_send, "xh", SWAP).astype(F32)).astype(BF16)
    outgoing, second = call(
        outgoing_kernel,
        [SMEM, VMEM, VMEM],
        (global_blocks, glob, w_sum.reshape(NZ, PIECE, DM // PIECE)),
        (shaped((NZ, PIECE, 2 * HALF + DM // PIECE)), shaped((NZ, PIECE, 2 * HALF))),
    )
    owned = over_columns(outgoing)
    second = lax.cond(clash, over_columns, lambda _: nothing, second)
    from_upper = lax.ppermute(to_lower, "z", DOWN)
    from_lower = lax.ppermute(to_upper, "z", UP)
    kv_mine, back = call(
        combine_kernel,
        [SMEM] + [VMEM] * 6,
        (
            global_blocks, dq, own, from_upper, from_lower,
            owned.reshape(BLK, -1), second.reshape(BLK, -1),
        ),
        (shaped((BLK, 2 * HALF)), shaped((BLK, 3 * HALF))),
    )
    w_row = jnp.sum(owned[:, :, 2 * HALF :].astype(F32), axis=0)
    w_row = lax.ppermute(w_row, ("xh", "xl"), CROSS)
    full = shaped((BLK, 2 * HALF))
    query_grad, key_grad, value_grad, w_row = call(
        final_kernel,
        [VMEM] * 4,
        (dq, kv_mine, lax.ppermute(back, "xl", SWAP), w_row),
        (full, full, full, shaped(w_row.shape, F32)),
    )
    return query_grad[None], key_grad[None], value_grad[None], w_row.reshape(1, DM)


def solution(mesh):
    fine = Mesh(mesh.devices.reshape(2, NY, 2, 2, NZ), ("xh", "y", "c", "xl", "z"))
    dp, ctx = ("xh", "y", "c"), ("xl", "z")
    frames = P(dp, ctx, None)
    return jax.shard_map(
        on_device,
        mesh=fine,
        in_specs=(frames, frames, frames, frames, P(dp, None), P(), P()),
        out_specs=(frames, frames, frames, P(dp + ctx, None)),
        check_vma=False,
    )
```

```python
import jax
import jax.numpy as jnp
from jax import lax
from jax.experimental import pallas as pl
from jax.experimental.pallas import tpu as pltpu
from jax.sharding import Mesh, PartitionSpec as P

HDIM = 128
BLK = 128
HALF = 256
NZ = 16
NY = 4
NCTX = 32
PIECE = 8
NGLOB = 3
DM = 1024
SCALE = HDIM ** (-0.5)

UP = [(i, (i + 1) % NZ) for i in range(NZ)]
DOWN = [(i, (i - 1) % NZ) for i in range(NZ)]
SWAP = [(0, 1), (1, 0)]

CROSS = [(0, 0), (1, 2), (2, 1), (3, 3)]

Y_ONE = [(i, i ^ 1) for i in range(NY)]
Y_TWO = [(i, i ^ 2) for i in range(NY)]

VMEM = pl.BlockSpec(memory_space=pltpu.VMEM)
SMEM = pl.BlockSpec(memory_space=pltpu.SMEM)
ANY = pl.BlockSpec(memory_space=pl.ANY)
HBM = pl.BlockSpec(memory_space=pltpu.HBM)
BF16, F32 = jnp.bfloat16, jnp.float32


def shaped(shape, dtype=BF16):
    return jax.ShapeDtypeStruct(shape, dtype)


def call(kernel, specs, operands, out_shape, scratch=(), flops=0, nbytes=2**20, vmem=8):
    return pl.pallas_call(
        kernel,
        out_shape=out_shape,
        in_specs=specs,
        out_specs=jax.tree.map(lambda _: VMEM, out_shape),
        scratch_shapes=scratch,
        compiler_params=pltpu.CompilerParams(vmem_limit_bytes=vmem * 2**20),
        cost_estimate=pl.CostEstimate(flops=flops, bytes_accessed=nbytes, transcendentals=0),
    )(*operands)


def rows_dot(left, right):
    return lax.dot_general(left, right, (((0,), (0,)), ((), ())), preferred_element_type=F32)


def cols_dot(left, right):
    return lax.dot_general(left, right, (((1,), (1,)), ((), ())), preferred_element_type=F32)


def shard_rows(i, j):
    y = lax.axis_index("y") ^ i
    core = lax.axis_index("c") ^ j
    return pl.ds(pl.multiple_of((y * 2 + core) * NCTX, NCTX), NCTX)


def split_kernel(q_hbm, k_hbm, v_hbm, halves_ref, mine_ref, send_ref, parts, sems):
    first = lax.axis_index("xl") == 0
    copies = [
        pltpu.make_async_copy(ref, parts.at[i], sems.at[i])
        for i, ref in enumerate((k_hbm, v_hbm, q_hbm))
    ]
    for copy in copies:
        copy.start()
    for part in range(3):
        copies[part].wait()
        ref = parts.at[part]
        low, high = ref[:, :HALF], ref[:, HALF:]
        lanes = slice(part * HALF, (part + 1) * HALF)
        if part < 2:
            halves_ref[0, :, lanes] = low
            halves_ref[1, :, lanes] = high
        mine_ref[:, lanes] = jnp.where(first, low, high)
        send_ref[:, lanes] = jnp.where(first, high, low)


def is_global(globals_ref, block):
    found = block == globals_ref[0]
    for g in range(1, NGLOB):
        found = found | (block == globals_ref[g])
    return found


def place(globals_ref, g):
    block = globals_ref[g]
    second = (block >= NZ) & is_global(globals_ref, block - NZ)
    return jnp.where(block >= NZ, block - NZ, block), second


def first_slot(globals_ref):
    lower_slot = lax.axis_index("xl")
    return jnp.where(is_global(globals_ref, lax.axis_index("z")), lower_slot, 1 - lower_slot)


def stack_kernel(mine_ref, other_ref, kv_ref):
    kv_ref[0] = mine_ref[:, : 2 * HALF]
    kv_ref[1] = other_ref[:, : 2 * HALF]


def choose_kernel(globals_ref, pieces_ref, *refs):
    chosen_ref = refs[-1]
    for g in range(NGLOB):
        piece = pieces_ref[globals_ref[g]]
        for z in range(NZ):
            chosen_ref[z, :, g * 2 * HALF : (g + 1) * 2 * HALF] = piece


def project_kernel(grad_ref, grad_other_ref, w_ref, w_other_ref, d_ref, d_other_ref, w_scr):
    for j, ref in enumerate((w_ref, w_other_ref)):
        for i in range(NY):
            w_scr[shard_rows(i, j)] = ref[i * NCTX : (i + 1) * NCTX]
    d_ref[...] = cols_dot(grad_ref[...], w_scr[...]).astype(BF16)
    d_other_ref[...] = cols_dot(grad_other_ref[...], w_scr[...]).astype(BF16)


def attention_kernel(
    tiles_ref, globals_ref, mine_ref, other_ref, before_ref, after_ref, shared_ref,
    d_mine_ref, d_other_ref, grad_ref, grad_other_ref,
    dq_ref, own_ref, lower_ref, upper_ref, glob_ref, keep_ref, send_ref, attended_ref,
    projected_ref,
):
    xl = lax.axis_index("xl")
    z = lax.axis_index("z")
    for slot in range(2):
        block = (xl if slot == 0 else 1 - xl) * NZ + z
        kvq_ref = mine_ref if slot == 0 else other_ref
        d_ref = d_mine_ref if slot == 0 else d_other_ref
        below = jnp.where(z == 0, 1 - slot, slot)
        above = jnp.where(z == NZ - 1, 1 - slot, slot)
        seen = []
        for column in range(3):
            other = block + column - 1
            is_global = other == globals_ref[0]
            for g in range(1, NGLOB):
                is_global = is_global | (other == globals_ref[g])
            listed = tiles_ref[block, column] > 0
            seen.append((other >= 0) & (other < NCTX) & listed & jnp.logical_not(is_global))
        chunk = lax.broadcasted_iota(jnp.int32, (1, 6 * BLK), 1) // BLK
        mask = chunk >= 3
        for column in range(3):
            mask = mask | ((chunk == column) & seen[column])
        for head in range(2):
            lanes = slice(head * HDIM, (head + 1) * HDIM)
            v_lanes = slice(HALF + head * HDIM, HALF + (head + 1) * HDIM)
            q_lanes = slice(2 * HALF + head * HDIM, 2 * HALF + (head + 1) * HDIM)
            q_head = kvq_ref[:, q_lanes]
            d_head = d_ref[:, lanes]

            def gathered(at):
                parts = [before_ref[below, :, at], kvq_ref[:, at], after_ref[above, :, at]]
                for g in range(NGLOB):
                    start = g * 2 * HALF + at.start
                    parts.append(shared_ref[:, start : start + HDIM])
                return jnp.concatenate(parts, 0)

            keys, vals = gathered(lanes), gathered(v_lanes)
            scores = jnp.where(mask, cols_dot(q_head, keys) * SCALE, -jnp.inf)
            peak = jnp.max(scores, axis=1, keepdims=True)
            expo = jnp.exp(scores - peak)
            prob = expo / jnp.sum(expo, axis=1, keepdims=True)
            prob_low = prob.astype(BF16)
            out = jnp.dot(prob_low, vals, preferred_element_type=F32).astype(BF16)
            attended_ref[slot * BLK : (slot + 1) * BLK, lanes] = out
            delta = jnp.sum(d_head.astype(F32) * out.astype(F32), axis=1, keepdims=True)
            dscore = (prob * (cols_dot(d_head, vals) - delta)).astype(BF16)
            dq = SCALE * jnp.dot(dscore, keys, preferred_element_type=F32)
            dq_ref[slot, :, lanes] = dq.astype(BF16)
            for at, grad in (
                (lanes, SCALE * rows_dot(dscore, q_head)),
                (v_lanes, rows_dot(prob_low, d_head)),
            ):
                lower_ref[below, :, at] = grad[:BLK].astype(BF16)
                own_ref[slot, :, at] = grad[BLK : 2 * BLK]
                upper_ref[above, :, at] = grad[2 * BLK : 3 * BLK].astype(BF16)
                for g in range(NGLOB):
                    start = g * 2 * HALF + at.start
                    part = grad[(3 + g) * BLK : (4 + g) * BLK]
                    if slot == 0:
                        glob_ref[:, start : start + HDIM] = part
                    else:
                        glob_ref[:, start : start + HDIM] += part
    projected_ref[...] = rows_dot(attended_ref[:BLK], grad_ref[...])
    projected_ref[...] += rows_dot(attended_ref[BLK:], grad_other_ref[...])
    for i in range(NY):
        keep_ref[i] = projected_ref[shard_rows(i, 0)]
        send_ref[i] = projected_ref[shard_rows(i, 1)].astype(BF16)


def attention_call(*operands):
    def kernel(*refs):
        ins, outs, scratch = refs[:11], refs[11:18], refs[18:]
        glob_out, rest = outs[4], scratch
        attention_kernel(*ins, *outs[:4], rest[0], outs[5], outs[6], rest[1], rest[2])
        glob_out[...] = rest[0][...].astype(BF16)

    out_shape = (
        shaped((2, BLK, HALF)),
        shaped((2, BLK, 2 * HALF), F32),
        shaped((2, BLK, 2 * HALF)),
        shaped((2, BLK, 2 * HALF)),
        shaped((BLK, NGLOB * 2 * HALF)),
        shaped((NY, NCTX, DM), F32),
        shaped((NY, NCTX, DM)),
    )
    return pl.pallas_call(
        kernel,
        out_shape=out_shape,
        in_specs=[SMEM] * 2 + [VMEM] * 9,
        out_specs=(VMEM,) * len(out_shape),
        scratch_shapes=[
            pltpu.VMEM((BLK, NGLOB * 2 * HALF), F32),
            pltpu.VMEM((2 * BLK, HALF), BF16),
            pltpu.VMEM((HALF, DM), F32),
        ],
        compiler_params=pltpu.CompilerParams(vmem_limit_bytes=24 * 2**20),
        cost_estimate=pl.CostEstimate(
            flops=10**9, bytes_accessed=5 * 2**20, transcendentals=400000
        ),
    )(*operands)


def outgoing_kernel(globals_ref, glob_ref, w_ref, out_ref, second_ref):
    total = glob_ref[0].astype(F32)
    for z in range(1, NZ):
        total += glob_ref[z].astype(F32)
    out_ref[:, :, : 2 * HALF] = jnp.zeros((NZ, PIECE, 2 * HALF), BF16)
    out_ref[:, :, 2 * HALF :] = w_ref[...]
    second_ref[...] = jnp.zeros((NZ, PIECE, 2 * HALF), BF16)
    for g in range(NGLOB):
        part = total[:, g * 2 * HALF : (g + 1) * 2 * HALF].astype(BF16)
        column, second = place(globals_ref, g)

        @pl.when(second)
        def _():
            second_ref[column] = part

        @pl.when(jnp.logical_not(second))
        def _():
            out_ref[column, :, : 2 * HALF] = part


def combine_kernel(
    globals_ref, dq_ref, own_ref, upper_ref, lower_ref, owned_ref, second_ref, kv_ref, back_ref
):
    first = first_slot(globals_ref)
    upper_slot = 1 - lax.axis_index("xl")
    owned = owned_ref[:, : 2 * HALF].astype(F32)
    second = second_ref[...].astype(F32)
    for slot in range(2):
        total = own_ref[slot] + upper_ref[slot].astype(F32) + lower_ref[slot].astype(F32)
        total += jnp.where(first == slot, owned, 0.0)
        total += jnp.where(upper_slot == slot, second, 0.0)
        if slot == 0:
            kv_ref[...] = total.astype(BF16)
        else:
            back_ref[:, HALF:] = total.astype(BF16)
            back_ref[:, :HALF] = dq_ref[1]


def final_kernel(dq_ref, kv_ref, back_ref, w_ref, q_ref, k_ref, v_ref, w_out_ref):
    w_out_ref[...] = w_ref[...]
    first = lax.axis_index("xl") == 0
    for half in range(2):
        mine = first if half == 0 else jnp.logical_not(first)
        lanes = slice(half * HALF, (half + 1) * HALF)
        q_ref[:, lanes] = jnp.where(mine, dq_ref[0], back_ref[:, :HALF])
        k_ref[:, lanes] = jnp.where(mine, kv_ref[:, :HALF], back_ref[:, HALF : 2 * HALF])
        v_ref[:, lanes] = jnp.where(mine, kv_ref[:, HALF:], back_ref[:, 2 * HALF :])


def over_columns(array):
    return lax.all_to_all(array.reshape(NZ, PIECE, -1), "z", 0, 0, tiled=True)


def on_device(query, key, value, out_grad, w_out, band_tiles, global_blocks):
    xl = lax.axis_index("xl")
    q, k, v, grad = query[0], key[0], value[0], out_grad[0]

    folded = global_blocks % NZ
    clash = (
        (folded[0] == folded[1]) | (folded[0] == folded[2]) | (folded[1] == folded[2])
    )
    nothing = jnp.zeros((NZ, PIECE, 2 * HALF), BF16)

    halves, mine, send = call(
        split_kernel,
        [HBM] * 3,
        (q, k, v),
        (shaped((2, BLK, 2 * HALF)), shaped((BLK, 3 * HALF)), shaped((BLK, 3 * HALF))),
        [pltpu.VMEM((3, BLK, 2 * HALF), BF16), pltpu.SemaphoreType.DMA((3,))],
        vmem=56,
    )
    pieces = lax.all_to_all(
        halves.reshape(NCTX, PIECE, 2 * HALF), ("xl", "z"), 0, 0, tiled=True
    )
    other = lax.ppermute(send, "xl", SWAP)
    grad_other = lax.ppermute(grad, "xl", SWAP)
    w0 = lax.ppermute(w_out, ("xh", "xl"), CROSS)
    w1 = lax.ppermute(w0, "y", Y_ONE)
    kv = call(stack_kernel, [VMEM] * 2, (mine, other), shaped((2, BLK, 2 * HALF)))
    before = lax.ppermute(kv, "z", UP)
    after = lax.ppermute(kv, "z", DOWN)
    chosen = call(
        choose_kernel,
        [SMEM, VMEM] + [ANY] * 4,
        (global_blocks, pieces, before, after, w0, grad_other),
        shaped((NZ, PIECE, NGLOB * 2 * HALF)),
    )
    shared = over_columns(chosen).reshape(BLK, NGLOB * 2 * HALF)
    w01 = jnp.concatenate([w0, w1], 0)
    w_core = jnp.concatenate([w01, lax.ppermute(w01, "y", Y_TWO)], 0)
    d_mine, d_other = call(
        project_kernel,
        [VMEM] * 4,
        (grad, grad_other, w_core, lax.ppermute(w_core, "c", SWAP)),
        (shaped((BLK, HALF)), shaped((BLK, HALF))),
        [pltpu.VMEM((HALF, DM), BF16)],
    )

    dq, own, to_lower, to_upper, glob, w_keep, w_send = attention_call(
        band_tiles, global_blocks, mine, other, before, after, shared,
        d_mine, d_other, grad, grad_other,
    )

    glob = over_columns(glob)
    w_sum = w_keep + lax.ppermute(w_send, "c", SWAP).astype(F32)
    w_sum = w_sum[:2] + lax.ppermute(w_sum[2:].astype(BF16), "y", Y_TWO).astype(F32)
    w_sum = w_sum[0] + lax.ppermute(w_sum[1].astype(BF16), "y", Y_ONE).astype(F32)
    lower = lax.axis_index("xh") == 0
    w_send = jnp.where(lower, w_sum[NZ:], w_sum[:NZ]).astype(BF16)
    w_sum = jnp.where(lower, w_sum[:NZ], w_sum[NZ:])
    w_sum = (w_sum + lax.ppermute(w_send, "xh", SWAP).astype(F32)).astype(BF16)
    outgoing, second = call(
        outgoing_kernel,
        [SMEM, VMEM, VMEM],
        (global_blocks, glob, w_sum.reshape(NZ, PIECE, DM // PIECE)),
        (shaped((NZ, PIECE, 2 * HALF + DM // PIECE)), shaped((NZ, PIECE, 2 * HALF))),
    )
    owned = over_columns(outgoing)
    second = lax.cond(clash, over_columns, lambda _: nothing, second)
    from_upper = lax.ppermute(to_lower, "z", DOWN)
    from_lower = lax.ppermute(to_upper, "z", UP)
    kv_mine, back = call(
        combine_kernel,
        [SMEM] + [VMEM] * 6,
        (
            global_blocks, dq, own, from_upper, from_lower,
            owned.reshape(BLK, -1), second.reshape(BLK, -1),
        ),
        (shaped((BLK, 2 * HALF)), shaped((BLK, 3 * HALF))),
    )
    w_row = jnp.sum(owned[:, :, 2 * HALF :].astype(F32), axis=0)
    w_row = lax.ppermute(w_row, ("xh", "xl"), CROSS)
    full = shaped((BLK, 2 * HALF))
    query_grad, key_grad, value_grad, w_row = call(
        final_kernel,
        [VMEM] * 4,
        (dq, kv_mine, lax.ppermute(back, "xl", SWAP), w_row),
        (full, full, full, shaped(w_row.shape, F32)),
    )
    return query_grad[None], key_grad[None], value_grad[None], w_row.reshape(1, DM)


def solution(mesh):
    fine = Mesh(mesh.devices.reshape(2, NY, 2, 2, NZ), ("xh", "y", "c", "xl", "z"))
    dp, ctx = ("xh", "y", "c"), ("xl", "z")
    frames = P(dp, ctx, None)
    return jax.shard_map(
        on_device,
        mesh=fine,
        in_specs=(frames, frames, frames, frames, P(dp, None), P(), P()),
        out_specs=(frames, frames, frames, P(dp + ctx, None)),
        check_vma=False,
    )
```
